32 devices in a mesh: group: 2 (over y), dp: 8 (over z, x), fsdp: 2 (over core).
Axes of the slice: x: 2, y: 2, z: 4, core: 2. Of those that a mesh axis runs over, the one named last changes fastest.
Arguments:
- patches: bfloat16 [4, 3584, 1536], P(('group', 'fsdp'), 'dp'), parts along dimension 0, may hold values from -6 to 6
- ln_gain: float32 [1536], replicated, may hold values from 0.25 to 1.75
- ln_bias: float32 [1536], replicated, may hold values from -3 to 3
- qkv_weight: bfloat16 [1536, 4608], P(None, ('dp', 'fsdp')), may hold values from -0.15625 to 0.15625
- qkv_bias: float32 [4608], replicated, may hold values from -7 to 7
- lengths: int32 [4, 8, 8], P(('group', 'fsdp')), parts along dimension 0, may hold values from 14 to 56, as said below
- destinations: int32 [4, 8, 8], P(('group', 'fsdp')), parts along dimension 0, may hold values from 0 to 7, each once within a row
Outputs:
- context: bfloat16 [4, 3584, 1536], P(('group', 'fsdp'), 'dp'), parts along dimension 0
The draws below stay inside these ranges and needn't reach their ends.
There are 2 independent parts, one for each index of `group`. The reference program is written for one: setup_inputs(seed, part) draws one part's arguments, and reference() takes and returns one part's arrays. A program takes and returns all parts, laid end to end along the dimension named above; an argument that names none is the same for every part. Nothing has to cross between parts.
Inputs may be any that keep to these rules, and one draw needn't show every extreme that they name: `lengths`: between 14 and 56; each device's row reaches 56. `destinations`: each device sends exactly one image to every dp index, itself included.
All inputs are finite; a program needn't handle non-finite values.
Results may differ from the reference program's by a relative error of at most 0.0024.
The reference program's roundings to bfloat16 on the way count: a program that leaves them out, or rounds other values in their place, can miss the bound.
Values may be sent and summed in bfloat16 or wider, within the bound.
A program may use at most 128 MiB of HBM per device.

```python
import jax
import jax.numpy as jnp
from jax import lax

D = 1536
HEADS = 24
HEAD = 64
CAP = 56
ROWS = 448
N_DP = 8
N_FSDP = 2


def draw_lengths(key, part):
    key = jax.random.fold_in(key, 11)
    first, second = jax.random.split(key)
    values = jax.random.randint(first, (N_FSDP, N_DP, N_DP), CAP // 4, CAP + 1)
    where_top = jax.random.randint(second, (N_FSDP, N_DP, 1), 0, N_DP)
    pos = jnp.arange(N_DP)[None, None, :]
    return jnp.where(pos == where_top, CAP, values).astype(jnp.int32)


def draw_qkv_bias(key, part):
    key = jax.random.fold_in(key, 23)
    first = jax.random.fold_in(key, 0)
    values = 0.5 * jax.random.normal(first, (3 * D,), jnp.float32)
    return jnp.clip(values, -3.0, 3.0).astype(jnp.float32)


def levels(key, dims, pieces, low, largest):
    gain, own = 1.0, jax.random.fold_in(key, 6)
    for position, shards_of in pieces:
        steps = jnp.exp(jax.random.uniform(jax.random.fold_in(own, position), (shards_of,), jnp.float32, low / len(pieces), largest / len(pieces)))
        gain = gain * jnp.repeat(steps, dims[position] // shards_of).reshape([-1 if axis == position else 1 for axis in range(len(dims))])
    return gain


def normal_values(own_key, shape, width, limit, cuts=(), held_as=jnp.bfloat16):
    values = jax.random.normal(own_key, shape, jnp.float32) * width
    if len(cuts) > 0:
        values = levels(own_key, shape, cuts, -0.22, 0.18) * values
    return jnp.clip(values, min=-limit, max=limit).astype(held_as)


def setup_inputs(seed: int = 0, part: int = 0) -> dict:
    splits = jax.random.split(jax.random.key(seed), 8)
    part_splits = jax.random.split(jax.random.fold_in(splits[7], part), 8)
    return {
        "patches": normal_values(part_splits[0], (N_FSDP, N_DP * ROWS, D), 1.0, 6.0, ((0, 2), (1, 8))),
        "ln_gain": jnp.clip(1.0 + 0.15 * jax.random.normal(splits[1], (D,), jnp.float32), 0.25, 1.75),
        "ln_bias": normal_values(splits[2], (D,), 0.5, 3.0, (), jnp.float32),
        "qkv_weight": normal_values(splits[3], (D, 3 * D), D ** -0.5, 0.15625, ((1, 16),)),
        "qkv_bias": draw_qkv_bias(jax.random.fold_in(splits[7], 71), part),
        "lengths": draw_lengths(jax.random.fold_in(jax.random.fold_in(splits[7], part), 71), part),
        "destinations": jax.vmap(lambda own: jax.random.permutation(own, N_DP))(jax.random.split(part_splits[6], N_FSDP * N_DP)).reshape((N_FSDP, N_DP, N_DP)).astype(jnp.int32),
    }


def attend(got, lens, ln_gain, ln_bias, qkv_weight, qkv_bias):
    flat = got.reshape(N_DP * CAP, D).astype(jnp.float32)
    mean = lax.optimization_barrier(jnp.mean(flat, axis=1, keepdims=True))
    centred = flat - mean
    var = lax.optimization_barrier(jnp.mean(centred * centred, axis=1, keepdims=True))
    normed = (centred * lax.rsqrt(var + 1e-06) * ln_gain + ln_bias).astype(jnp.bfloat16)
    qkv = (jnp.dot(normed, qkv_weight, preferred_element_type=jnp.float32) + qkv_bias).astype(jnp.bfloat16)
    query = qkv[:, :D].reshape(N_DP, CAP, HEADS, HEAD).astype(jnp.float32)
    keys = qkv[:, D:2 * D].reshape(N_DP, CAP, HEADS, HEAD).astype(jnp.float32)
    values = qkv[:, 2 * D:].reshape(N_DP, CAP, HEADS, HEAD).astype(jnp.float32)
    scores = jnp.einsum('sqhe,skhe->shqk', query, keys) * HEAD ** (-0.5)
    pos = jnp.arange(CAP, dtype=jnp.int32)
    live = pos[None, :] < lens[:, None]
    scores = jnp.where(live[:, None, None, :], scores, jnp.float32(-1e+30))
    top = lax.optimization_barrier(jnp.max(scores, axis=3, keepdims=True))
    expo = jnp.exp(scores - top)
    probs = (expo / lax.optimization_barrier(jnp.sum(expo, axis=3, keepdims=True))).astype(jnp.bfloat16)
    ctx = jnp.einsum('shqk,skhe->sqhe', probs.astype(jnp.float32), values)
    ctx = jnp.where(live[:, :, None, None], ctx, jnp.float32(0.0))
    return ctx.reshape(N_DP * CAP, D).astype(jnp.bfloat16)

def reference(patches, ln_gain, ln_bias, qkv_weight, qkv_bias, lengths, destinations):

    def column(packed):
        rows, lens, dests = packed
        source = rows.reshape(N_DP, N_DP * CAP, D)
        offs = jnp.cumsum(lens, axis=1) - lens
        hit = dests[:, None, :] == jnp.arange(N_DP, dtype=jnp.int32)[None, :, None]
        slot_len = lax.optimization_barrier(jnp.sum(jnp.where(hit, lens[:, None, :], 0), axis=2)).astype(jnp.int32)
        slot_off = lax.optimization_barrier(jnp.sum(jnp.where(hit, offs[:, None, :], 0), axis=2)).astype(jnp.int32)

        def one_dest(dest):
            lens_d = lax.dynamic_index_in_dim(slot_len, dest, 1, keepdims=False)
            offs_d = lax.dynamic_index_in_dim(slot_off, dest, 1, keepdims=False)
            pos = jnp.arange(CAP, dtype=jnp.int32)
            live = pos[None, :] < lens_d[:, None]
            index = jnp.where(live, offs_d[:, None] + pos[None, :], 0).astype(jnp.int32)
            got = jnp.take_along_axis(source, index[:, :, None], axis=1)
            got = jnp.where(live[:, :, None], got, jnp.zeros((), got.dtype))
            return attend(got, lens_d, ln_gain, ln_bias, qkv_weight, qkv_bias)
        return lax.map(one_dest, jnp.arange(N_DP, dtype=jnp.int32))
    out = lax.map(column, (patches, lengths, destinations))
    return out.reshape(N_FSDP, N_DP * N_DP * CAP, D)
```

```python
import functools

import jax
import jax.numpy as jnp
from jax import lax
from jax.experimental import pallas as pl
from jax.experimental.pallas import tpu as pltpu
from jax.sharding import PartitionSpec as P

HEAD = 64
GROUP = 4
COLS = HEAD * GROUP
BF16 = jnp.bfloat16
F32 = jnp.float32


def attend_kernel(n_images, cap, len_ref, got_ref, gain_ref, shift_ref, bq_ref, bk_ref, bv_ref, wq_ref, wk_ref, wv_ref, out_ref, normed):
    @pl.when(pl.program_id(0) == 0)
    def _():
        for s in range(n_images):
            x = got_ref[s].astype(F32)
            centred = x - jnp.mean(x, axis=1, keepdims=True)
            var = jnp.mean(centred * centred, axis=1, keepdims=True)
            y = centred * lax.rsqrt(var + 1e-06) * gain_ref[...] + shift_ref[...]
            normed[s * cap : (s + 1) * cap, :] = y

    rows = normed[...].astype(BF16)

    def project(w_ref, b_ref):
        y = lax.dot_general(rows, w_ref[...], (((1,), (1,)), ((), ())), preferred_element_type=F32)
        return (y + b_ref[...]).astype(BF16).astype(F32)

    q, k, v = project(wq_ref, bq_ref), project(wk_ref, bk_ref), project(wv_ref, bv_ref)
    lane_head = lax.broadcasted_iota(jnp.int32, (cap, COLS), 1) // HEAD
    key_at = lax.broadcasted_iota(jnp.int32, (GROUP * cap, cap), 1)
    row_at = lax.broadcasted_iota(jnp.int32, (cap, COLS), 0)
    for s in range(n_images):
        at = slice(s * cap, (s + 1) * cap)
        length = len_ref[s]
        stacked = jnp.concatenate([jnp.where(lane_head == h, q[at], 0.0) for h in range(GROUP)], axis=0)
        scores = lax.dot_general(stacked.astype(BF16), k[at].astype(BF16), (((1,), (1,)), ((), ())), preferred_element_type=F32)
        scores = jnp.where(key_at < length, scores * HEAD ** (-0.5), -1e30)
        expo = jnp.exp(scores - jnp.max(scores, axis=1, keepdims=True))
        probs = (expo / jnp.sum(expo, axis=1, keepdims=True)).astype(BF16)
        mixed = jnp.dot(probs, v[at].astype(BF16), preferred_element_type=F32)
        total = jnp.where(lane_head == 0, mixed[:cap], 0.0)
        for h in range(1, GROUP):
            total = jnp.where(lane_head == h, mixed[h * cap : (h + 1) * cap], total)
        out_ref[s] = jnp.where(row_at < length, total, 0.0).astype(BF16)


def attend(got, recv_len, gain, shift, weight_t, bias):
    n_images, cap, width = got.shape
    steps = width // COLS
    full = lambda shape: pl.BlockSpec(shape, lambda i: (0,) * len(shape))
    bias_spec = lambda part: pl.BlockSpec((1, COLS), lambda i: (0, part * steps + i))
    weight_spec = lambda part: pl.BlockSpec((COLS, width), lambda i: (part * steps + i, 0))
    bias = bias.reshape(1, -1)
    return pl.pallas_call(
        functools.partial(attend_kernel, n_images, cap),
        grid=(steps,),
        in_specs=[
            pl.BlockSpec(memory_space=pltpu.SMEM),
            full((n_images, cap, width)),
            full((1, width)),
            full((1, width)),
            bias_spec(0),
            bias_spec(1),
            bias_spec(2),
            weight_spec(0),
            weight_spec(1),
            weight_spec(2),
        ],
        out_specs=pl.BlockSpec((n_images, cap, COLS), lambda i: (0, 0, i)),
        out_shape=jax.ShapeDtypeStruct((n_images, cap, width), BF16),
        scratch_shapes=[pltpu.VMEM((n_images * cap, width), F32)],
        compiler_params=pltpu.CompilerParams(vmem_limit_bytes=48 * 2**20),
        cost_estimate=pl.CostEstimate(flops=2 * n_images * cap * width * 3 * width, bytes_accessed=3 * width * width * 2, transcendentals=0),
    )(recv_len, got, gain.reshape(1, -1), shift.reshape(1, -1), bias, bias, bias, weight_t, weight_t, weight_t)


def move(patches, qkv_weight, table_len, table_dest):
    n_dp = lax.axis_size("dp")
    me_dp = lax.axis_index("dp")
    cap, width = patches.shape[0] // n_dp, patches.shape[1]
    own_len = lax.dynamic_index_in_dim(table_len, me_dp, 0, keepdims=False)
    own_dest = lax.dynamic_index_in_dim(table_dest, me_dp, 0, keepdims=False)
    offsets = jnp.cumsum(own_len) - own_len
    onehot = own_dest[None, :] == jnp.arange(n_dp, dtype=jnp.int32)[:, None]
    slot_len = jnp.sum(jnp.where(onehot, own_len[None, :], 0), axis=1)
    slot_off = jnp.sum(jnp.where(onehot, offsets[None, :], 0), axis=1)
    position = jnp.arange(cap, dtype=jnp.int32)
    live = position[None, :] < slot_len[:, None]
    index = jnp.where(live, slot_off[:, None] + position[None, :], 0)
    picked = jnp.take(patches, index.reshape(-1), axis=0).reshape(n_dp, cap, width)
    outgoing = jnp.where(live[:, :, None], picked, jnp.zeros((), picked.dtype))
    got = lax.all_to_all(outgoing, "dp", split_axis=0, concat_axis=0, tiled=True)
    weight_t = lax.all_gather(qkv_weight.T, ("dp", "fsdp"), axis=0, tiled=True)
    return got, weight_t


def on_device(patches, ln_gain, ln_bias, qkv_weight, qkv_bias, lengths, destinations):
    me_dp = lax.axis_index("dp")
    table_len, table_dest = lengths[0], destinations[0]
    got, weight_t = move(patches[0], qkv_weight, table_len, table_dest)
    recv_len = jnp.sum(jnp.where(table_dest == me_dp, table_len, 0), axis=1)
    context = attend(got, recv_len, ln_gain, ln_bias, weight_t, qkv_bias)
    return context.reshape(1, -1, context.shape[2])


def solution(mesh):
    placed = (
        P(("group", "fsdp"), "dp", None),
        P(),
        P(),
        P(None, ("dp", "fsdp")),
        P(),
        P(("group", "fsdp"), None, None),
        P(("group", "fsdp"), None, None),
    )
    return jax.shard_map(
        on_device,
        mesh=mesh,
        in_specs=placed,
        out_specs=P(("group", "fsdp"), "dp", None),
        check_vma=False,
    )
```

```python
import functools

import jax
import jax.numpy as jnp
from jax import lax
from jax.experimental import pallas as pl
from jax.experimental.pallas import tpu as pltpu
from jax.sharding import PartitionSpec as P

HEAD = 64
GROUP = 4
COLS = HEAD * GROUP
BF16 = jnp.bfloat16
F32 = jnp.float32


def attend_kernel(n_images, cap, len_ref, got_ref, gain_ref, shift_ref, bq_ref, bk_ref, bv_ref, wq_ref, wk_ref, wv_ref, out_ref, normed):
    @pl.when(pl.program_id(0) == 0)
    def _():
        for s in range(n_images):
            x = got_ref[s].astype(F32)
            centred = x - jnp.mean(x, axis=1, keepdims=True)
            var = jnp.mean(centred * centred, axis=1, keepdims=True)
            y = centred * lax.rsqrt(var + 1e-06) * gain_ref[...] + shift_ref[...]
            normed[s * cap : (s + 1) * cap, :] = y

    rows = normed[...].astype(BF16)

    def project(w_ref, b_ref):
        y = lax.dot_general(rows, w_ref[...], (((1,), (1,)), ((), ())), preferred_element_type=F32)
        return (y + b_ref[...]).astype(BF16).astype(F32)

    q, k, v = project(wq_ref, bq_ref), project(wk_ref, bk_ref), project(wv_ref, bv_ref)
    lane_head = lax.broadcasted_iota(jnp.int32, (cap, COLS), 1) // HEAD
    key_at = lax.broadcasted_iota(jnp.int32, (GROUP * cap, cap), 1)
    row_at = lax.broadcasted_iota(jnp.int32, (cap, COLS), 0)
    for s in range(n_images):
        at = slice(s * cap, (s + 1) * cap)
        length = len_ref[s]
        stacked = jnp.concatenate([jnp.where(lane_head == h, q[at], 0.0) for h in range(GROUP)], axis=0)
        scores = lax.dot_general(stacked.astype(BF16), k[at].astype(BF16), (((1,), (1,)), ((), ())), preferred_element_type=F32)
        scores = jnp.where(key_at < length, scores * HEAD ** (-0.5), -1e30)
        expo = jnp.exp(scores - jnp.max(scores, axis=1, keepdims=True))
        probs = (expo / jnp.sum(expo, axis=1, keepdims=True)).astype(BF16)
        mixed = jnp.dot(probs, v[at].astype(BF16), preferred_element_type=F32)
        total = jnp.where(lane_head == 0, mixed[:cap], 0.0)
        for h in range(1, GROUP):
            total = jnp.where(lane_head == h, mixed[h * cap : (h + 1) * cap], total)
        out_ref[s] = jnp.where(row_at < length, total, 0.0).astype(BF16)


def attend(got, recv_len, gain, shift, weight_t, bias):
    n_images, cap, width = got.shape
    steps = width // COLS
    full = lambda shape: pl.BlockSpec(shape, lambda i: (0,) * len(shape))
    bias_spec = lambda part: pl.BlockSpec((1, COLS), lambda i: (0, part * steps + i))
    weight_spec = lambda part: pl.BlockSpec((COLS, width), lambda i: (part * steps + i, 0))
    bias = bias.reshape(1, -1)
    return pl.pallas_call(
        functools.partial(attend_kernel, n_images, cap),
        grid=(steps,),
        in_specs=[
            pl.BlockSpec(memory_space=pltpu.SMEM),
            full((n_images, cap, width)),
            full((1, width)),
            full((1, width)),
            bias_spec(0),
            bias_spec(1),
            bias_spec(2),
            weight_spec(0),
            weight_spec(1),
            weight_spec(2),
        ],
        out_specs=pl.BlockSpec((n_images, cap, COLS), lambda i: (0, 0, i)),
        out_shape=jax.ShapeDtypeStruct((n_images, cap, width), BF16),
        scratch_shapes=[pltpu.VMEM((n_images * cap, width), F32)],
        compiler_params=pltpu.CompilerParams(vmem_limit_bytes=48 * 2**20),
        cost_estimate=pl.CostEstimate(flops=2 * n_images * cap * width * 3 * width, bytes_accessed=3 * width * width * 2, transcendentals=0),
    )(recv_len, got, gain.reshape(1, -1), shift.reshape(1, -1), bias, bias, bias, weight_t, weight_t, weight_t)


def move(patches, qkv_weight, table_len, table_dest):
    n_dp = lax.axis_size("dp")
    me_dp = lax.axis_index("dp")
    cap, width = patches.shape[0] // n_dp, patches.shape[1]
    own_len = lax.dynamic_index_in_dim(table_len, me_dp, 0, keepdims=False)
    own_dest = lax.dynamic_index_in_dim(table_dest, me_dp, 0, keepdims=False)
    offsets = jnp.cumsum(own_len) - own_len
    onehot = own_dest[None, :] == jnp.arange(n_dp, dtype=jnp.int32)[:, None]
    slot_len = jnp.sum(jnp.where(onehot, own_len[None, :], 0), axis=1)
    slot_off = jnp.sum(jnp.where(onehot, offsets[None, :], 0), axis=1)
    position = jnp.arange(cap, dtype=jnp.int32)
    live = position[None, :] < slot_len[:, None]
    index = jnp.where(live, slot_off[:, None] + position[None, :], 0)
    picked = jnp.take(patches, index.reshape(-1), axis=0).reshape(n_dp, cap, width)
    outgoing = jnp.where(live[:, :, None], picked, jnp.zeros((), picked.dtype))
    got = lax.all_to_all(outgoing, "dp", split_axis=0, concat_axis=0, tiled=True)
    weight_t = lax.all_gather(qkv_weight.T, ("dp", "fsdp"), axis=0, tiled=True)
    return got, weight_t


MESH = pl.DeviceIdType.MESH
PARTS = 3


def move_kernel(n_dp, cap, len_ref, dest_ref, rows_ref, shard_ref, got_ref, all_ref, outgoing, up_sem, down_sem, x_sem, y_sem, core_sem, ring_in, core_in, image_out, image_in, local_sem):
    group, dp, core = lax.axis_index("group"), lax.axis_index("dp"), lax.axis_index("fsdp")
    nz = n_dp // 2
    z = dp // 2
    across = dp + 1 - 2 * (dp % 2)
    own_parts = (2 * group, 1)
    other_part = 2 - 2 * group
    replica = (1 - group, dp, core)
    mate = (group, dp, 1 - core)

    barrier = pltpu.get_barrier_semaphore()
    for j in range(1, n_dp):
        pl.semaphore_signal(barrier, inc=1, device_id=(group, (dp + j) % n_dp, core), device_id_type=MESH)
    pl.semaphore_signal(barrier, inc=1, device_id=replica, device_id_type=MESH)
    pl.semaphore_signal(barrier, inc=1, device_id=mate, device_id_type=MESH)
    pl.semaphore_wait(barrier, n_dp + 1)

    sent = []

    def send(sems, into, who, part, device, own, *conditions):
        def copy():
            return pltpu.make_async_remote_copy(
                src_ref=shard_ref.at[part] if own else all_ref.at[who, core, part],
                dst_ref=all_ref.at[who, core, part],
                send_sem=sems.at[who, part],
                recv_sem=into.at[who, part],
                device_id=device,
                device_id_type=MESH,
            )

        when(conditions, lambda: copy().start())
        sent.append((conditions, lambda: copy().wait_send()))

    def when(conditions, do):
        if conditions:
            pl.when(conditions[0])(lambda: when(conditions[1:], do))
        else:
            do()

    def arrive(sems, who, of_core, part, *conditions):
        def wait():
            pltpu.make_async_remote_copy(
                src_ref=all_ref.at[who, of_core, part],
                dst_ref=all_ref.at[who, of_core, part],
                send_sem=y_sem.at[who, part],
                recv_sem=sems.at[who, part],
                device_id=mate,
                device_id_type=MESH,
            ).wait_recv()

        when(conditions, wait)

    for part in own_parts:
        send(up_sem, ring_in, dp, part, (group, dp + 2, core), True, z < nz - 1)
        send(down_sem, ring_in, dp, part, (group, dp - 2, core), True, z > 0)
        send(x_sem, ring_in, dp, part, (group, across, core), True)

    own_dest = [dest_ref[dp, i] for i in range(n_dp)]
    own_len = [len_ref[dp, i] for i in range(n_dp)]
    row_at = lax.broadcasted_iota(jnp.int32, (cap, n_dp * cap), 0)
    column_at = lax.broadcasted_iota(jnp.int32, (cap, n_dp * cap), 1)
    picks = []
    for j in range(n_dp):
        to = (dp + j) % n_dp
        length, offset, start = jnp.int32(0), jnp.int32(0), jnp.int32(0)
        for i in range(n_dp):
            length = jnp.where(own_dest[i] == to, own_len[i], length)
            offset = jnp.where(own_dest[i] == to, start, offset)
            start = start + own_len[i]
        picks.append(jnp.where((row_at < length) & (column_at == row_at + offset), 1.0, 0.0))
    pick = jnp.concatenate(picks, axis=0).astype(BF16)
    picked = jnp.dot(pick, rows_ref[...], preferred_element_type=F32)
    for j in range(n_dp):
        outgoing[j] = picked[j * cap : (j + 1) * cap].astype(BF16)

    def image(j):
        return pltpu.make_async_remote_copy(
            src_ref=outgoing.at[j],
            dst_ref=got_ref.at[dp],
            send_sem=image_out.at[j],
            recv_sem=image_in.at[j],
            device_id=(group, (dp + j) % n_dp, core),
            device_id_type=MESH,
        )

    def image_arrival(j):
        source = (dp + n_dp - j) % n_dp
        return pltpu.make_async_remote_copy(
            src_ref=outgoing.at[j],
            dst_ref=got_ref.at[source],
            send_sem=image_out.at[j],
            recv_sem=image_in.at[j],
            device_id=(group, source, core),
            device_id_type=MESH,
        )

    for j in range(1, n_dp):
        image(j).start()
    own_image = pltpu.make_async_copy(outgoing.at[0], got_ref.at[dp], local_sem.at[0])
    own_image.start()
    own_shard = pltpu.make_async_copy(shard_ref, all_ref.at[dp, core], local_sem.at[1])
    own_shard.start()
    for part in range(PARTS):
        send(core_sem, core_in, dp, part, mate, True)

    def sides(d):
        if d == 0:
            return [((), 0, 0)]
        return [((z >= d,), -2 * d, 1), ((z < nz - d,), 2 * d, -1)]

    def from_z(d):
        for at, part in enumerate(own_parts):
            for valid, step, way in sides(d):
                who = dp + step
                arrive(ring_in, who, core, part, *valid)
                if way == 1:
                    send(up_sem, ring_in, who, part, (group, dp + 2, core), False, *valid, z < nz - 1)
                else:
                    send(down_sem, ring_in, who, part, (group, dp - 2, core), False, *valid, z > 0)
                send(x_sem, ring_in, who, part, (group, across, core), False, *valid)
                if at == 0:
                    send(y_sem, ring_in, who, part, replica, False, *valid)
                send(core_sem, core_in, who, part, mate, False, *valid)

    def from_x(d):
        for at, part in enumerate(own_parts):
            for valid, step, _ in sides(d):
                who = across + step
                arrive(ring_in, who, core, part, *valid)
                if at == 0:
                    send(y_sem, ring_in, who, part, replica, False, *valid)
                send(core_sem, core_in, who, part, mate, False, *valid)

    def from_y(d, base):
        for valid, step, _ in sides(d):
            arrive(ring_in, base + step, core, other_part, *valid)
            send(core_sem, core_in, base + step, other_part, mate, False, *valid)

    for d in range(1, nz + 2):
        if d < nz:
            from_z(d)
        if d <= nz:
            from_x(d - 1)
        if 2 <= d <= nz:
            from_y(d - 1, dp)
        if d >= 2:
            from_y(d - 2, across)

    for who in range(n_dp):
        for part in range(PARTS):
            arrive(core_in, who, 1 - core, part)
    for j in range(1, n_dp):
        image_arrival(j).wait_recv()
    for conditions, wait in sent:
        when(conditions, wait)
    for j in range(1, n_dp):
        image(j).wait_send()
    own_image.wait()
    own_shard.wait()


def move_by_copies(patches, qkv_weight, table_len, table_dest):
    n_dp, n_core = lax.axis_size("dp"), lax.axis_size("fsdp")
    cap, width = patches.shape[0] // n_dp, patches.shape[1]
    columns = qkv_weight.shape[1]
    shard = qkv_weight.T.reshape(PARTS, columns // PARTS, width)
    dma = pltpu.SemaphoreType.DMA
    got, gathered = pl.pallas_call(
        functools.partial(move_kernel, n_dp, cap),
        in_specs=[
            pl.BlockSpec(memory_space=pltpu.SMEM),
            pl.BlockSpec(memory_space=pltpu.SMEM),
            pl.BlockSpec(memory_space=pltpu.VMEM),
            pl.BlockSpec(memory_space=pl.ANY),
        ],
        out_specs=[pl.BlockSpec(memory_space=pl.ANY)] * 2,
        out_shape=[
            jax.ShapeDtypeStruct((n_dp, cap, width), BF16),
            jax.ShapeDtypeStruct((n_dp, n_core, PARTS, columns // PARTS, width), BF16),
        ],
        scratch_shapes=[pltpu.VMEM((n_dp, cap, width), BF16)] + [dma((n_dp, PARTS))] * 7 + [dma((n_dp,))] * 2 + [dma((2,))],
        compiler_params=pltpu.CompilerParams(collective_id=0, has_side_effects=True, vmem_limit_bytes=40 * 2**20),
    )(table_len, table_dest, patches, shard)
    return got, gathered.reshape(n_dp * n_core * columns, width)


def on_device(patches, ln_gain, ln_bias, qkv_weight, qkv_bias, lengths, destinations):
    me_dp = lax.axis_index("dp")
    table_len, table_dest = lengths[0], destinations[0]
    by_copies = lax.axis_size("fsdp") == 2 and lax.axis_size("group") == 2 and lax.axis_size("dp") % 2 == 0
    got, weight_t = (move_by_copies if by_copies else move)(patches[0], qkv_weight, table_len, table_dest)
    recv_len = jnp.sum(jnp.where(table_dest == me_dp, table_len, 0), axis=1)
    context = attend(got, recv_len, ln_gain, ln_bias, weight_t, qkv_bias)
    return context.reshape(1, -1, context.shape[2])


def solution(mesh):
    placed = (
        P(("group", "fsdp"), "dp", None),
        P(),
        P(),
        P(None, ("dp", "fsdp")),
        P(),
        P(("group", "fsdp"), None, None),
        P(("group", "fsdp"), None, None),
    )
    return jax.shard_map(
        on_device,
        mesh=mesh,
        in_specs=placed,
        out_specs=P(("group", "fsdp"), "dp", None),
        check_vma=False,
    )
```

```python
import functools

import jax
import jax.numpy as jnp
from jax import lax
from jax.experimental import pallas as pl
from jax.experimental.pallas import tpu as pltpu
from jax.sharding import PartitionSpec as P

HEAD = 64
GROUP = 4
COLS = HEAD * GROUP
BF16 = jnp.bfloat16
F32 = jnp.float32


def attend_kernel(n_images, cap, table_len_ref, table_dest_ref, got_ref, gain_ref, shift_ref, bq_ref, bk_ref, bv_ref, wq_ref, wk_ref, wv_ref, out_ref, normed, len_ref):
    @pl.when(pl.program_id(0) == 0)
    def _():
        me = lax.axis_index("dp")
        for s in range(n_images):
            length = jnp.int32(0)
            for j in range(n_images):
                length = length + jnp.where(table_dest_ref[s, j] == me, table_len_ref[s, j], 0)
            len_ref[s] = length
        gain, shift = gain_ref[...][None, :], shift_ref[...][None, :]
        for s in range(0, n_images, 2):
            pair = []
            for x in (got_ref[s].astype(F32), got_ref[s + 1].astype(F32)):
                centred = x - jnp.mean(x, axis=1, keepdims=True)
                var = jnp.mean(centred * centred, axis=1, keepdims=True)
                pair.append(centred * lax.rsqrt(var + 1e-06) * gain + shift)
            normed[s * cap : (s + 2) * cap, :] = jnp.concatenate(pair, axis=0).astype(BF16)

    rows = normed[...]

    def project(w_ref, b_ref):
        y = lax.dot_general(rows, w_ref[...], (((1,), (1,)), ((), ())), preferred_element_type=F32)
        return (y + b_ref[...][None, :]).astype(BF16).astype(F32)

    q, k, v = project(wq_ref, bq_ref), project(wk_ref, bk_ref), project(wv_ref, bv_ref)
    lane_head = lax.broadcasted_iota(jnp.int32, (cap, COLS), 1) // HEAD
    key_at = lax.broadcasted_iota(jnp.int32, (cap, GROUP * cap), 0)
    row_at = lax.broadcasted_iota(jnp.int32, (cap, COLS), 0)
    for s in range(n_images):
        at = slice(s * cap, (s + 1) * cap)
        length = len_ref[s]
        stacked = jnp.concatenate([jnp.where(lane_head == h, q[at], 0.0) for h in range(GROUP)], axis=0)
        scores = lax.dot_general(k[at].astype(BF16), stacked.astype(BF16), (((1,), (1,)), ((), ())), preferred_element_type=F32)
        scores = jnp.where(key_at < length, scores * HEAD ** (-0.5), -1e30)
        expo = jnp.exp(scores - jnp.max(scores, axis=0, keepdims=True))
        probs = (expo * (1.0 / jnp.sum(expo, axis=0, keepdims=True))).astype(BF16)
        mixed = lax.dot_general(probs, v[at].astype(BF16), (((0,), (0,)), ((), ())), preferred_element_type=F32)
        total = jnp.where(lane_head == 0, mixed[:cap], 0.0)
        for h in range(1, GROUP):
            total = jnp.where(lane_head == h, mixed[h * cap : (h + 1) * cap], total)
        out_ref[s] = jnp.where(row_at < length, total, 0.0).astype(BF16)


def attend(got, table_len, table_dest, gain, shift, weight_t, bias):
    n_images, cap, width = got.shape
    steps = width // COLS
    full = lambda shape: pl.BlockSpec(shape, lambda i: (0,) * len(shape))
    bias_spec = lambda part: pl.BlockSpec((COLS,), lambda i: (part * steps + i,))
    weight_spec = lambda part: pl.BlockSpec((COLS, width), lambda i: (part * steps + i, 0))
    return pl.pallas_call(
        functools.partial(attend_kernel, n_images, cap),
        grid=(steps,),
        in_specs=[
            pl.BlockSpec(memory_space=pltpu.SMEM),
            pl.BlockSpec(memory_space=pltpu.SMEM),
            full((n_images, cap, width)),
            full((width,)),
            full((width,)),
            bias_spec(0),
            bias_spec(1),
            bias_spec(2),
            weight_spec(0),
            weight_spec(1),
            weight_spec(2),
        ],
        out_specs=pl.BlockSpec((n_images, cap, COLS), lambda i: (0, 0, i)),
        out_shape=jax.ShapeDtypeStruct((n_images, cap, width), BF16),
        scratch_shapes=[pltpu.VMEM((n_images * cap, width), BF16), pltpu.SMEM((n_images,), jnp.int32)],
        compiler_params=pltpu.CompilerParams(vmem_limit_bytes=48 * 2**20),
        cost_estimate=pl.CostEstimate(flops=2 * n_images * cap * width * 3 * width, bytes_accessed=3 * width * width * 2, transcendentals=0),
    )(table_len, table_dest, got, gain, shift, bias, bias, bias, weight_t, weight_t, weight_t)


def move(patches, qkv_weight, table_len, table_dest):
    n_dp = lax.axis_size("dp")
    me_dp = lax.axis_index("dp")
    cap, width = patches.shape[0] // n_dp, patches.shape[1]
    own_len = lax.dynamic_index_in_dim(table_len, me_dp, 0, keepdims=False)
    own_dest = lax.dynamic_index_in_dim(table_dest, me_dp, 0, keepdims=False)
    offsets = jnp.cumsum(own_len) - own_len
    onehot = own_dest[None, :] == jnp.arange(n_dp, dtype=jnp.int32)[:, None]
    slot_len = jnp.sum(jnp.where(onehot, own_len[None, :], 0), axis=1)
    slot_off = jnp.sum(jnp.where(onehot, offsets[None, :], 0), axis=1)
    position = jnp.arange(cap, dtype=jnp.int32)
    live = position[None, :] < slot_len[:, None]
    index = jnp.where(live, slot_off[:, None] + position[None, :], 0)
    picked = jnp.take(patches, index.reshape(-1), axis=0).reshape(n_dp, cap, width)
    outgoing = jnp.where(live[:, :, None], picked, jnp.zeros((), picked.dtype))
    got = lax.all_to_all(outgoing, "dp", split_axis=0, concat_axis=0, tiled=True)
    weight_t = lax.all_gather(qkv_weight.T, ("dp", "fsdp"), axis=0, tiled=True)
    return got, weight_t


MESH = pl.DeviceIdType.MESH
PARTS = 3


def move_kernel(n_dp, cap, len_ref, dest_ref, rows_ref, shard_ref, got_ref, all_ref, outgoing, up_sem, down_sem, x_sem, y_sem, core_sem, ring_in, core_in, image_out, image_in, local_sem):
    group, dp, core = lax.axis_index("group"), lax.axis_index("dp"), lax.axis_index("fsdp")
    nz = n_dp // 2
    z = dp // 2
    across = dp + 1 - 2 * (dp % 2)
    own_parts = (2 * group, 1)
    other_part = 2 - 2 * group
    replica = (1 - group, dp, core)
    mate = (group, dp, 1 - core)

    barrier = pltpu.get_barrier_semaphore()
    for j in range(1, n_dp):
        pl.semaphore_signal(barrier, inc=1, device_id=(group, (dp + j) % n_dp, core), device_id_type=MESH)
    pl.semaphore_signal(barrier, inc=1, device_id=replica, device_id_type=MESH)
    pl.semaphore_signal(barrier, inc=1, device_id=mate, device_id_type=MESH)
    pl.semaphore_wait(barrier, n_dp + 1)

    sent = []

    def send(sems, into, who, part, device, own, *conditions):
        def copy():
            return pltpu.make_async_remote_copy(
                src_ref=shard_ref.at[part] if own else all_ref.at[who, core, part],
                dst_ref=all_ref.at[who, core, part],
                send_sem=sems.at[who, part],
                recv_sem=into.at[who, part],
                device_id=device,
                device_id_type=MESH,
            )

        when(conditions, lambda: copy().start())
        sent.append((conditions, lambda: copy().wait_send()))

    def when(conditions, do):
        if conditions:
            pl.when(conditions[0])(lambda: when(conditions[1:], do))
        else:
            do()

    def arrive(sems, who, of_core, part, *conditions):
        def wait():
            pltpu.make_async_remote_copy(
                src_ref=all_ref.at[who, of_core, part],
                dst_ref=all_ref.at[who, of_core, part],
                send_sem=y_sem.at[who, part],
                recv_sem=sems.at[who, part],
                device_id=mate,
                device_id_type=MESH,
            ).wait_recv()

        when(conditions, wait)

    for part in own_parts:
        send(up_sem, ring_in, dp, part, (group, dp + 2, core), True, z < nz - 1)
        send(down_sem, ring_in, dp, part, (group, dp - 2, core), True, z > 0)
        send(x_sem, ring_in, dp, part, (group, across, core), True)

    own_dest = [dest_ref[dp, i] for i in range(n_dp)]
    own_len = [len_ref[dp, i] for i in range(n_dp)]
    row_at = lax.broadcasted_iota(jnp.int32, (cap, n_dp * cap), 0)
    column_at = lax.broadcasted_iota(jnp.int32, (cap, n_dp * cap), 1)
    picks = []
    for j in range(n_dp):
        to = (dp + j) % n_dp
        length, offset, start = jnp.int32(0), jnp.int32(0), jnp.int32(0)
        for i in range(n_dp):
            length = jnp.where(own_dest[i] == to, own_len[i], length)
            offset = jnp.where(own_dest[i] == to, start, offset)
            start = start + own_len[i]
        picks.append(jnp.where((row_at < length) & (column_at == row_at + offset), 1.0, 0.0))
    pick = jnp.concatenate(picks, axis=0).astype(BF16)
    picked = jnp.dot(pick, rows_ref[...], preferred_element_type=F32)
    for j in range(n_dp):
        outgoing[j] = picked[j * cap : (j + 1) * cap].astype(BF16)

    def image(j):
        return pltpu.make_async_remote_copy(
            src_ref=outgoing.at[j],
            dst_ref=got_ref.at[dp],
            send_sem=image_out.at[j],
            recv_sem=image_in.at[j],
            device_id=(group, (dp + j) % n_dp, core),
            device_id_type=MESH,
        )

    def image_arrival(j):
        source = (dp + n_dp - j) % n_dp
        return pltpu.make_async_remote_copy(
            src_ref=outgoing.at[j],
            dst_ref=got_ref.at[source],
            send_sem=image_out.at[j],
            recv_sem=image_in.at[j],
            device_id=(group, source, core),
            device_id_type=MESH,
        )

    for j in range(1, n_dp):
        image(j).start()
    own_image = pltpu.make_async_copy(outgoing.at[0], got_ref.at[dp], local_sem.at[0])
    own_image.start()
    own_shard = pltpu.make_async_copy(shard_ref, all_ref.at[dp, core], local_sem.at[1])
    own_shard.start()
    for part in range(PARTS):
        send(core_sem, core_in, dp, part, mate, True)

    def sides(d):
        if d == 0:
            return [((), 0, 0)]
        return [((z >= d,), -2 * d, 1), ((z < nz - d,), 2 * d, -1)]

    def from_z(d):
        for at, part in enumerate(own_parts):
            for valid, step, way in sides(d):
                who = dp + step
                arrive(ring_in, who, core, part, *valid)
                if way == 1:
                    send(up_sem, ring_in, who, part, (group, dp + 2, core), False, *valid, z < nz - 1)
                else:
                    send(down_sem, ring_in, who, part, (group, dp - 2, core), False, *valid, z > 0)
                send(x_sem, ring_in, who, part, (group, across, core), False, *valid)
                if at == 0:
                    send(y_sem, ring_in, who, part, replica, False, *valid)
                send(core_sem, core_in, who, part, mate, False, *valid)

    def from_x(d):
        for at, part in enumerate(own_parts):
            for valid, step, _ in sides(d):
                who = across + step
                arrive(ring_in, who, core, part, *valid)
                if at == 0:
                    send(y_sem, ring_in, who, part, replica, False, *valid)
                send(core_sem, core_in, who, part, mate, False, *valid)

    def from_y(d, base):
        for valid, step, _ in sides(d):
            arrive(ring_in, base + step, core, other_part, *valid)
            send(core_sem, core_in, base + step, other_part, mate, False, *valid)

    for d in range(1, nz + 2):
        if d < nz:
            from_z(d)
        if d <= nz:
            from_x(d - 1)
        if 2 <= d <= nz:
            from_y(d - 1, dp)
        if d >= 2:
            from_y(d - 2, across)

    for who in range(n_dp):
        for part in range(PARTS):
            arrive(core_in, who, 1 - core, part)
    for j in range(1, n_dp):
        image_arrival(j).wait_recv()
    for conditions, wait in sent:
        when(conditions, wait)
    for j in range(1, n_dp):
        image(j).wait_send()
    own_image.wait()
    own_shard.wait()


def move_by_copies(patches, qkv_weight, table_len, table_dest):
    n_dp, n_core = lax.axis_size("dp"), lax.axis_size("fsdp")
    cap, width = patches.shape[0] // n_dp, patches.shape[1]
    columns = qkv_weight.shape[1]
    shard = qkv_weight.T.reshape(PARTS, columns // PARTS, width)
    dma = pltpu.SemaphoreType.DMA
    got, gathered = pl.pallas_call(
        functools.partial(move_kernel, n_dp, cap),
        in_specs=[
            pl.BlockSpec(memory_space=pltpu.SMEM),
            pl.BlockSpec(memory_space=pltpu.SMEM),
            pl.BlockSpec(memory_space=pltpu.VMEM),
            pl.BlockSpec(memory_space=pl.ANY),
        ],
        out_specs=[pl.BlockSpec(memory_space=pl.ANY)] * 2,
        out_shape=[
            jax.ShapeDtypeStruct((n_dp, cap, width), BF16),
            jax.ShapeDtypeStruct((n_dp, n_core, PARTS, columns // PARTS, width), BF16),
        ],
        scratch_shapes=[pltpu.VMEM((n_dp, cap, width), BF16)] + [dma((n_dp, PARTS))] * 7 + [dma((n_dp,))] * 2 + [dma((2,))],
        compiler_params=pltpu.CompilerParams(collective_id=0, has_side_effects=True, vmem_limit_bytes=40 * 2**20),
    )(table_len, table_dest, patches, shard)
    return got, gathered.reshape(n_dp * n_core * columns, width)


def on_device(patches, ln_gain, ln_bias, qkv_weight, qkv_bias, lengths, destinations):
    table_len, table_dest = lengths[0], destinations[0]
    by_copies = lax.axis_size("fsdp") == 2 and lax.axis_size("group") == 2 and lax.axis_size("dp") % 2 == 0
    got, weight_t = (move_by_copies if by_copies else move)(patches[0], qkv_weight, table_len, table_dest)
    context = attend(got, table_len, table_dest, ln_gain, ln_bias, weight_t, qkv_bias)
    return context.reshape(1, -1, context.shape[2])


def solution(mesh):
    placed = (
        P(("group", "fsdp"), "dp", None),
        P(),
        P(),
        P(None, ("dp", "fsdp")),
        P(),
        P(("group", "fsdp"), None, None),
        P(("group", "fsdp"), None, None),
    )
    return jax.shard_map(
        on_device,
        mesh=mesh,
        in_specs=placed,
        out_specs=P(("group", "fsdp"), "dp", None),
        check_vma=False,
    )
```

```python
import functools

import jax
import jax.numpy as jnp
from jax import lax
from jax.experimental import pallas as pl
from jax.experimental.pallas import tpu as pltpu
from jax.sharding import PartitionSpec as P

HEAD = 64
GROUP = 4
COLS = HEAD * GROUP
BF16 = jnp.bfloat16
F32 = jnp.float32


def attend_kernel(n_images, cap, table_len_ref, table_dest_ref, got_ref, gain_ref, shift_ref, bq_ref, bk_ref, bv_ref, wq_ref, wk_ref, wv_ref, out_ref, normed, len_ref):
    @pl.when(pl.program_id(0) == 0)
    def _():
        me = lax.axis_index("dp")
        for s in range(n_images):
            length = jnp.int32(0)
            for j in range(n_images):
                length = length + jnp.where(table_dest_ref[s, j] == me, table_len_ref[s, j], 0)
            len_ref[s] = length
        gain, shift = gain_ref[...][None, :], shift_ref[...][None, :]
        for s in range(0, n_images, 2):
            pair = []
            for x in (got_ref[s].astype(F32), got_ref[s + 1].astype(F32)):
                centred = x - jnp.mean(x, axis=1, keepdims=True)
                var = jnp.mean(centred * centred, axis=1, keepdims=True)
                pair.append(centred * lax.rsqrt(var + 1e-06) * gain + shift)
            normed[s * cap : (s + 2) * cap, :] = jnp.concatenate(pair, axis=0).astype(BF16)

    rows = normed[...]

    def project(w_ref, b_ref):
        y = lax.dot_general(rows, w_ref[...], (((1,), (1,)), ((), ())), preferred_element_type=F32)
        return (y + b_ref[...][None, :]).astype(BF16).astype(F32)

    q, k, v = project(wq_ref, bq_ref), project(wk_ref, bk_ref), project(wv_ref, bv_ref)
    lane_head = lax.broadcasted_iota(jnp.int32, (cap, COLS), 1) // HEAD
    key_at = lax.broadcasted_iota(jnp.int32, (cap, GROUP * cap), 0)
    row_at = lax.broadcasted_iota(jnp.int32, (cap, COLS), 0)
    for s in range(n_images):
        at = slice(s * cap, (s + 1) * cap)
        length = len_ref[s]
        stacked = jnp.concatenate([jnp.where(lane_head == h, q[at], 0.0) for h in range(GROUP)], axis=0)
        scores = lax.dot_general(k[at].astype(BF16), stacked.astype(BF16), (((1,), (1,)), ((), ())), preferred_element_type=F32)
        scores = jnp.where(key_at < length, scores * HEAD ** (-0.5), -1e30)
        expo = jnp.exp(scores - jnp.max(scores, axis=0, keepdims=True))
        probs = (expo * (1.0 / jnp.sum(expo, axis=0, keepdims=True))).astype(BF16)
        mixed = lax.dot_general(probs, v[at].astype(BF16), (((0,), (0,)), ((), ())), preferred_element_type=F32)
        total = jnp.where(lane_head == 0, mixed[:cap], 0.0)
        for h in range(1, GROUP):
            total = jnp.where(lane_head == h, mixed[h * cap : (h + 1) * cap], total)
        out_ref[s] = jnp.where(row_at < length, total, 0.0).astype(BF16)


def attend(got, table_len, table_dest, gain, shift, weight_t, bias):
    n_images, cap, width = got.shape
    steps = width // COLS
    full = lambda shape: pl.BlockSpec(shape, lambda i: (0,) * len(shape))
    bias_spec = lambda part: pl.BlockSpec((COLS,), lambda i: (part * steps + i,))
    weight_spec = lambda part: pl.BlockSpec((COLS, width), lambda i: (part * steps + i, 0))
    return pl.pallas_call(
        functools.partial(attend_kernel, n_images, cap),
        grid=(steps,),
        in_specs=[
            pl.BlockSpec(memory_space=pltpu.SMEM),
            pl.BlockSpec(memory_space=pltpu.SMEM),
            full((n_images, cap, width)),
            full((width,)),
            full((width,)),
            bias_spec(0),
            bias_spec(1),
            bias_spec(2),
            weight_spec(0),
            weight_spec(1),
            weight_spec(2),
        ],
        out_specs=pl.BlockSpec((n_images, cap, COLS), lambda i: (0, 0, i)),
        out_shape=jax.ShapeDtypeStruct((n_images, cap, width), BF16),
        scratch_shapes=[pltpu.VMEM((n_images * cap, width), BF16), pltpu.SMEM((n_images,), jnp.int32)],
        compiler_params=pltpu.CompilerParams(vmem_limit_bytes=48 * 2**20),
        cost_estimate=pl.CostEstimate(flops=2 * n_images * cap * width * 3 * width, bytes_accessed=3 * width * width * 2, transcendentals=0),
    )(table_len, table_dest, got, gain, shift, bias, bias, bias, weight_t, weight_t, weight_t)


def move(patches, qkv_weight, table_len, table_dest):
    n_dp = lax.axis_size("dp")
    me_dp = lax.axis_index("dp")
    cap, width = patches.shape[0] // n_dp, patches.shape[1]
    own_len = lax.dynamic_index_in_dim(table_len, me_dp, 0, keepdims=False)
    own_dest = lax.dynamic_index_in_dim(table_dest, me_dp, 0, keepdims=False)
    offsets = jnp.cumsum(own_len) - own_len
    onehot = own_dest[None, :] == jnp.arange(n_dp, dtype=jnp.int32)[:, None]
    slot_len = jnp.sum(jnp.where(onehot, own_len[None, :], 0), axis=1)
    slot_off = jnp.sum(jnp.where(onehot, offsets[None, :], 0), axis=1)
    position = jnp.arange(cap, dtype=jnp.int32)
    live = position[None, :] < slot_len[:, None]
    index = jnp.where(live, slot_off[:, None] + position[None, :], 0)
    picked = jnp.take(patches, index.reshape(-1), axis=0).reshape(n_dp, cap, width)
    outgoing = jnp.where(live[:, :, None], picked, jnp.zeros((), picked.dtype))
    got = lax.all_to_all(outgoing, "dp", split_axis=0, concat_axis=0, tiled=True)
    weight_t = lax.all_gather(qkv_weight.T, ("dp", "fsdp"), axis=0, tiled=True)
    return got, weight_t


MESH = pl.DeviceIdType.MESH
PARTS = 3


def move_kernel(n_dp, cap, len_ref, dest_ref, rows_ref, shard_ref, got_ref, all_ref, outgoing, up_sem, down_sem, x_sem, y_sem, core_sem, ring_in, core_in, image_out, image_in, local_sem):
    group, dp, core = lax.axis_index("group"), lax.axis_index("dp"), lax.axis_index("fsdp")
    nz = n_dp // 2
    z = dp // 2
    across = dp + 1 - 2 * (dp % 2)
    own_parts = (2 * group, 1)
    other_part = 2 - 2 * group
    replica = (1 - group, dp, core)
    mate = (group, dp, 1 - core)

    barrier = pltpu.get_barrier_semaphore()
    for j in range(1, n_dp):
        pl.semaphore_signal(barrier, inc=1, device_id=(group, (dp + j) % n_dp, core), device_id_type=MESH)
    pl.semaphore_signal(barrier, inc=1, device_id=replica, device_id_type=MESH)
    pl.semaphore_signal(barrier, inc=1, device_id=mate, device_id_type=MESH)
    pl.semaphore_wait(barrier, n_dp + 1)

    sent = []

    def send(sems, into, who, part, device, own, *conditions):
        def copy():
            return pltpu.make_async_remote_copy(
                src_ref=shard_ref.at[part] if own else all_ref.at[who, core, part],
                dst_ref=all_ref.at[who, core, part],
                send_sem=sems.at[who, part],
                recv_sem=into.at[who, part],
                device_id=device,
                device_id_type=MESH,
            )

        when(conditions, lambda: copy().start())
        sent.append((conditions, lambda: copy().wait_send()))

    def by_x(at, d):
        return () if at == 0 else ((z + d) % 2 == group,)

    def when(conditions, do):
        if conditions:
            pl.when(conditions[0])(lambda: when(conditions[1:], do))
        else:
            do()

    def arrive(sems, who, of_core, part, *conditions):
        def wait():
            pltpu.make_async_remote_copy(
                src_ref=all_ref.at[who, of_core, part],
                dst_ref=all_ref.at[who, of_core, part],
                send_sem=y_sem.at[who, part],
                recv_sem=sems.at[who, part],
                device_id=mate,
                device_id_type=MESH,
            ).wait_recv()

        when(conditions, wait)

    for at, part in enumerate(own_parts):
        send(up_sem, ring_in, dp, part, (group, dp + 2, core), True, z < nz - 1)
        send(down_sem, ring_in, dp, part, (group, dp - 2, core), True, z > 0)
        send(x_sem, ring_in, dp, part, (group, across, core), True, *by_x(at, 0))

    own_dest = [dest_ref[dp, i] for i in range(n_dp)]
    own_len = [len_ref[dp, i] for i in range(n_dp)]
    row_at = lax.broadcasted_iota(jnp.int32, (cap, n_dp * cap), 0)
    column_at = lax.broadcasted_iota(jnp.int32, (cap, n_dp * cap), 1)
    picks = []
    for j in range(n_dp):
        to = (dp + j) % n_dp
        length, offset, start = jnp.int32(0), jnp.int32(0), jnp.int32(0)
        for i in range(n_dp):
            length = jnp.where(own_dest[i] == to, own_len[i], length)
            offset = jnp.where(own_dest[i] == to, start, offset)
            start = start + own_len[i]
        picks.append(jnp.where((row_at < length) & (column_at == row_at + offset), 1.0, 0.0))
    pick = jnp.concatenate(picks, axis=0).astype(BF16)
    picked = jnp.dot(pick, rows_ref[...], preferred_element_type=F32)
    for j in range(n_dp):
        outgoing[j] = picked[j * cap : (j + 1) * cap].astype(BF16)

    def image(j):
        return pltpu.make_async_remote_copy(
            src_ref=outgoing.at[j],
            dst_ref=got_ref.at[dp],
            send_sem=image_out.at[j],
            recv_sem=image_in.at[j],
            device_id=(group, (dp + j) % n_dp, core),
            device_id_type=MESH,
        )

    def image_arrival(j):
        source = (dp + n_dp - j) % n_dp
        return pltpu.make_async_remote_copy(
            src_ref=outgoing.at[j],
            dst_ref=got_ref.at[source],
            send_sem=image_out.at[j],
            recv_sem=image_in.at[j],
            device_id=(group, source, core),
            device_id_type=MESH,
        )

    for j in range(1, n_dp):
        image(j).start()
    own_image = pltpu.make_async_copy(outgoing.at[0], got_ref.at[dp], local_sem.at[0])
    own_image.start()
    own_shard = pltpu.make_async_copy(shard_ref, all_ref.at[dp, core], local_sem.at[1])
    own_shard.start()
    for part in range(PARTS):
        send(core_sem, core_in, dp, part, mate, True)

    def sides(d):
        if d == 0:
            return [((), 0, 0)]
        return [((z >= d,), -2 * d, 1), ((z < nz - d,), 2 * d, -1)]

    def from_z(d):
        for at, part in enumerate(own_parts):
            for valid, step, way in sides(d):
                who = dp + step
                arrive(ring_in, who, core, part, *valid)
                if way == 1:
                    send(up_sem, ring_in, who, part, (group, dp + 2, core), False, *valid, z < nz - 1)
                else:
                    send(down_sem, ring_in, who, part, (group, dp - 2, core), False, *valid, z > 0)
                send(x_sem, ring_in, who, part, (group, across, core), False, *valid, *by_x(at, d))
                if at == 0:
                    send(y_sem, ring_in, who, part, replica, False, *valid)
                send(core_sem, core_in, who, part, mate, False, *valid)

    def from_x(d):
        for at, part in enumerate(own_parts):
            for valid, step, _ in sides(d):
                who = across + step
                valid = valid + by_x(at, d)
                arrive(ring_in, who, core, part, *valid)
                send(y_sem, ring_in, who, part, replica, False, *valid)
                send(core_sem, core_in, who, part, mate, False, *valid)

    def from_y(d, base):
        for valid, step, _ in sides(d):
            who = base + step
            arrive(ring_in, who, core, other_part, *valid)
            send(core_sem, core_in, who, other_part, mate, False, *valid)
            if base is across:
                valid = valid + ((z + d) % 2 != group,)
                arrive(ring_in, who, core, 1, *valid)
                send(core_sem, core_in, who, 1, mate, False, *valid)

    for d in range(1, nz + 2):
        if d < nz:
            from_z(d)
        if d <= nz:
            from_x(d - 1)
        if 2 <= d <= nz:
            from_y(d - 1, dp)
        if d >= 2:
            from_y(d - 2, across)

    for who in range(n_dp):
        for part in range(PARTS):
            arrive(core_in, who, 1 - core, part)
    for j in range(1, n_dp):
        image_arrival(j).wait_recv()
    for conditions, wait in sent:
        when(conditions, wait)
    for j in range(1, n_dp):
        image(j).wait_send()
    own_image.wait()
    own_shard.wait()


def move_by_copies(patches, qkv_weight, table_len, table_dest):
    n_dp, n_core = lax.axis_size("dp"), lax.axis_size("fsdp")
    cap, width = patches.shape[0] // n_dp, patches.shape[1]
    columns = qkv_weight.shape[1]
    shard = qkv_weight.T.reshape(PARTS, columns // PARTS, width)
    dma = pltpu.SemaphoreType.DMA
    got, gathered = pl.pallas_call(
        functools.partial(move_kernel, n_dp, cap),
        in_specs=[
            pl.BlockSpec(memory_space=pltpu.SMEM),
            pl.BlockSpec(memory_space=pltpu.SMEM),
            pl.BlockSpec(memory_space=pltpu.VMEM),
            pl.BlockSpec(memory_space=pl.ANY),
        ],
        out_specs=[pl.BlockSpec(memory_space=pl.ANY)] * 2,
        out_shape=[
            jax.ShapeDtypeStruct((n_dp, cap, width), BF16),
            jax.ShapeDtypeStruct((n_dp, n_core, PARTS, columns // PARTS, width), BF16),
        ],
        scratch_shapes=[pltpu.VMEM((n_dp, cap, width), BF16)] + [dma((n_dp, PARTS))] * 7 + [dma((n_dp,))] * 2 + [dma((2,))],
        compiler_params=pltpu.CompilerParams(collective_id=0, has_side_effects=True, vmem_limit_bytes=40 * 2**20),
    )(table_len, table_dest, patches, shard)
    return got, gathered.reshape(n_dp * n_core * columns, width)


def on_device(patches, ln_gain, ln_bias, qkv_weight, qkv_bias, lengths, destinations):
    table_len, table_dest = lengths[0], destinations[0]
    by_copies = lax.axis_size("fsdp") == 2 and lax.axis_size("group") == 2 and lax.axis_size("dp") % 2 == 0
    got, weight_t = (move_by_copies if by_copies else move)(patches[0], qkv_weight, table_len, table_dest)
    context = attend(got, table_len, table_dest, ln_gain, ln_bias, weight_t, qkv_bias)
    return context.reshape(1, -1, context.shape[2])


def solution(mesh):
    placed = (
        P(("group", "fsdp"), "dp", None),
        P(),
        P(),
        P(None, ("dp", "fsdp")),
        P(),
        P(("group", "fsdp"), None, None),
        P(("group", "fsdp"), None, None),
    )
    return jax.shard_map(
        on_device,
        mesh=mesh,
        in_specs=placed,
        out_specs=P(("group", "fsdp"), "dp", None),
        check_vma=False,
    )
```

```python
import functools

import jax
import jax.numpy as jnp
from jax import lax
from jax.experimental import pallas as pl
from jax.experimental.pallas import tpu as pltpu
from jax.sharding import PartitionSpec as P

HEAD = 64
GROUP = 4
COLS = HEAD * GROUP
BF16 = jnp.bfloat16
F32 = jnp.float32


def attend_kernel(n_images, cap, table_len_ref, table_dest_ref, got_ref, gain_ref, shift_ref, bq_ref, bk_ref, bv_ref, wq_ref, wk_ref, wv_ref, out_ref, normed, len_ref):
    @pl.when(pl.program_id(0) == 0)
    def _():
        me = lax.axis_index("dp")
        for s in range(n_images):
            length = jnp.int32(0)
            for j in range(n_images):
                length = length + jnp.where(table_dest_ref[s, j] == me, table_len_ref[s, j], 0)
            len_ref[s] = length
        gain, shift = gain_ref[...][None, :], shift_ref[...][None, :]
        for s in range(0, n_images, 2):
            pair = []
            for x in (got_ref[s].astype(F32), got_ref[s + 1].astype(F32)):
                centred = x - jnp.mean(x, axis=1, keepdims=True)
                var = jnp.mean(centred * centred, axis=1, keepdims=True)
                pair.append(centred * lax.rsqrt(var + 1e-06) * gain + shift)
            normed[s * cap : (s + 2) * cap, :] = jnp.concatenate(pair, axis=0).astype(BF16)

    rows = normed[...]

    def project(w_ref, b_ref):
        y = lax.dot_general(rows, w_ref[...], (((1,), (1,)), ((), ())), preferred_element_type=F32)
        return (y + b_ref[...][None, :]).astype(BF16).astype(F32)

    q, k, v = project(wq_ref, bq_ref), project(wk_ref, bk_ref), project(wv_ref, bv_ref)
    lane_head = lax.broadcasted_iota(jnp.int32, (cap, COLS), 1) // HEAD
    key_at = lax.broadcasted_iota(jnp.int32, (cap, GROUP * cap), 0)
    row_at = lax.broadcasted_iota(jnp.int32, (cap, COLS), 0)
    for s in range(n_images):
        at = slice(s * cap, (s + 1) * cap)
        length = len_ref[s]
        stacked = jnp.concatenate([jnp.where(lane_head == h, q[at], 0.0) for h in range(GROUP)], axis=0)
        scores = lax.dot_general(k[at].astype(BF16), stacked.astype(BF16), (((1,), (1,)), ((), ())), preferred_element_type=F32)
        scores = jnp.where(key_at < length, scores * HEAD ** (-0.5), -1e30)
        expo = jnp.exp(scores - jnp.max(scores, axis=0, keepdims=True))
        probs = (expo * (1.0 / jnp.sum(expo, axis=0, keepdims=True))).astype(BF16)
        mixed = lax.dot_general(probs, v[at].astype(BF16), (((0,), (0,)), ((), ())), preferred_element_type=F32)
        total = jnp.where(lane_head == 0, mixed[:cap], 0.0)
        for h in range(1, GROUP):
            total = jnp.where(lane_head == h, mixed[h * cap : (h + 1) * cap], total)
        out_ref[s] = jnp.where(row_at < length, total, 0.0).astype(BF16)


def attend(got, table_len, table_dest, gain, shift, weight_t, bias):
    n_images, cap, width = got.shape
    steps = width // COLS
    full = lambda shape: pl.BlockSpec(shape, lambda i: (0,) * len(shape))
    bias_spec = lambda part: pl.BlockSpec((COLS,), lambda i: (part * steps + i,))
    weight_spec = lambda part: pl.BlockSpec((COLS, width), lambda i: (part * steps + i, 0))
    return pl.pallas_call(
        functools.partial(attend_kernel, n_images, cap),
        grid=(steps,),
        in_specs=[
            pl.BlockSpec(memory_space=pltpu.SMEM),
            pl.BlockSpec(memory_space=pltpu.SMEM),
            full((n_images, cap, width)),
            full((width,)),
            full((width,)),
            bias_spec(0),
            bias_spec(1),
            bias_spec(2),
            weight_spec(0),
            weight_spec(1),
            weight_spec(2),
        ],
        out_specs=pl.BlockSpec((n_images, cap, COLS), lambda i: (0, 0, i)),
        out_shape=jax.ShapeDtypeStruct((n_images, cap, width), BF16),
        scratch_shapes=[pltpu.VMEM((n_images * cap, width), BF16), pltpu.SMEM((n_images,), jnp.int32)],
        compiler_params=pltpu.CompilerParams(vmem_limit_bytes=48 * 2**20),
        cost_estimate=pl.CostEstimate(flops=2 * n_images * cap * width * 3 * width, bytes_accessed=3 * width * width * 2, transcendentals=0),
    )(table_len, table_dest, got, gain, shift, bias, bias, bias, weight_t, weight_t, weight_t)


def move(patches, qkv_weight, table_len, table_dest):
    n_dp = lax.axis_size("dp")
    me_dp = lax.axis_index("dp")
    cap, width = patches.shape[0] // n_dp, patches.shape[1]
    own_len = lax.dynamic_index_in_dim(table_len, me_dp, 0, keepdims=False)
    own_dest = lax.dynamic_index_in_dim(table_dest, me_dp, 0, keepdims=False)
    offsets = jnp.cumsum(own_len) - own_len
    onehot = own_dest[None, :] == jnp.arange(n_dp, dtype=jnp.int32)[:, None]
    slot_len = jnp.sum(jnp.where(onehot, own_len[None, :], 0), axis=1)
    slot_off = jnp.sum(jnp.where(onehot, offsets[None, :], 0), axis=1)
    position = jnp.arange(cap, dtype=jnp.int32)
    live = position[None, :] < slot_len[:, None]
    index = jnp.where(live, slot_off[:, None] + position[None, :], 0)
    picked = jnp.take(patches, index.reshape(-1), axis=0).reshape(n_dp, cap, width)
    outgoing = jnp.where(live[:, :, None], picked, jnp.zeros((), picked.dtype))
    got = lax.all_to_all(outgoing, "dp", split_axis=0, concat_axis=0, tiled=True)
    weight_t = lax.all_gather(qkv_weight.T, ("dp", "fsdp"), axis=0, tiled=True)
    return got, weight_t


MESH = pl.DeviceIdType.MESH
PARTS = 3


def move_kernel(n_dp, cap, len_ref, dest_ref, rows_ref, shard_ref, got_ref, all_ref, outgoing, up_sem, down_sem, x_sem, y_sem, core_sem, ring_in, core_in, image_out, image_in, local_sem):
    group, dp, core = lax.axis_index("group"), lax.axis_index("dp"), lax.axis_index("fsdp")
    nz = n_dp // 2
    z = dp // 2
    across = dp + 1 - 2 * (dp % 2)
    own_parts = (2 * group, 1)
    other_part = 2 - 2 * group
    replica = (1 - group, dp, core)
    mate = (group, dp, 1 - core)

    barrier = pltpu.get_barrier_semaphore()
    for j in range(1, n_dp):
        pl.semaphore_signal(barrier, inc=1, device_id=(group, (dp + j) % n_dp, core), device_id_type=MESH)
    pl.semaphore_signal(barrier, inc=1, device_id=replica, device_id_type=MESH)
    pl.semaphore_signal(barrier, inc=1, device_id=mate, device_id_type=MESH)
    pl.semaphore_wait(barrier, n_dp + 1)

    sent = []

    def send(sems, into, who, part, device, own, *conditions):
        def copy():
            return pltpu.make_async_remote_copy(
                src_ref=shard_ref.at[part] if own else all_ref.at[who, core, part],
                dst_ref=all_ref.at[who, core, part],
                send_sem=sems.at[who, part],
                recv_sem=into.at[who, part],
                device_id=device,
                device_id_type=MESH,
            )

        when(conditions, lambda: copy().start())
        sent.append((conditions, lambda: copy().wait_send()))

    def when(conditions, do):
        if conditions:
            pl.when(conditions[0])(lambda: when(conditions[1:], do))
        else:
            do()

    def arrive(sems, who, of_core, part, *conditions):
        def wait():
            pltpu.make_async_remote_copy(
                src_ref=all_ref.at[who, of_core, part],
                dst_ref=all_ref.at[who, of_core, part],
                send_sem=y_sem.at[who, part],
                recv_sem=sems.at[who, part],
                device_id=mate,
                device_id_type=MESH,
            ).wait_recv()

        when(conditions, wait)

    for part in own_parts:
        send(up_sem, ring_in, dp, part, (group, dp + 2, core), True, z < nz - 1)
        send(down_sem, ring_in, dp, part, (group, dp - 2, core), True, z > 0)
        send(x_sem, ring_in, dp, part, (group, across, core), True)

    own_dest = [dest_ref[dp, i] for i in range(n_dp)]
    own_len = [len_ref[dp, i] for i in range(n_dp)]
    row_at = lax.broadcasted_iota(jnp.int32, (cap, n_dp * cap), 0)
    column_at = lax.broadcasted_iota(jnp.int32, (cap, n_dp * cap), 1)
    picks = []
    for j in range(n_dp):
        to = (dp + j) % n_dp
        length, offset, start = jnp.int32(0), jnp.int32(0), jnp.int32(0)
        for i in range(n_dp):
            length = jnp.where(own_dest[i] == to, own_len[i], length)
            offset = jnp.where(own_dest[i] == to, start, offset)
            start = start + own_len[i]
        picks.append(jnp.where((row_at < length) & (column_at == row_at + offset), 1.0, 0.0))
    pick = jnp.concatenate(picks, axis=0).astype(BF16)
    picked = jnp.dot(pick, rows_ref[...], preferred_element_type=F32)
    for j in range(n_dp):
        outgoing[j] = picked[j * cap : (j + 1) * cap].astype(BF16)

    def image(j):
        return pltpu.make_async_remote_copy(
            src_ref=outgoing.at[j],
            dst_ref=got_ref.at[dp],
            send_sem=image_out.at[j],
            recv_sem=image_in.at[j],
            device_id=(group, (dp + j) % n_dp, core),
            device_id_type=MESH,
        )

    def image_arrival(j):
        source = (dp + n_dp - j) % n_dp
        return pltpu.make_async_remote_copy(
            src_ref=outgoing.at[j],
            dst_ref=got_ref.at[source],
            send_sem=image_out.at[j],
            recv_sem=image_in.at[j],
            device_id=(group, source, core),
            device_id_type=MESH,
        )

    own_image = pltpu.make_async_copy(outgoing.at[0], got_ref.at[dp], local_sem.at[0])
    own_image.start()
    own_shard = pltpu.make_async_copy(shard_ref, all_ref.at[dp, core], local_sem.at[1])
    own_shard.start()
    for part in range(PARTS):
        send(core_sem, core_in, dp, part, mate, True)

    def sides(d):
        if d == 0:
            return [((), 0, 0)]
        return [((z >= d,), -2 * d, 1), ((z < nz - d,), 2 * d, -1)]

    def from_z(d):
        for at, part in enumerate(own_parts):
            for valid, step, way in sides(d):
                who = dp + step
                arrive(ring_in, who, core, part, *valid)
                if way == 1:
                    send(up_sem, ring_in, who, part, (group, dp + 2, core), False, *valid, z < nz - 1)
                else:
                    send(down_sem, ring_in, who, part, (group, dp - 2, core), False, *valid, z > 0)
                send(x_sem, ring_in, who, part, (group, across, core), False, *valid)
                if at == 0:
                    send(y_sem, ring_in, who, part, replica, False, *valid)
                send(core_sem, core_in, who, part, mate, False, *valid)

    def from_x(d):
        for at, part in enumerate(own_parts):
            for valid, step, _ in sides(d):
                who = across + step
                arrive(ring_in, who, core, part, *valid)
                if at == 0:
                    send(y_sem, ring_in, who, part, replica, False, *valid)
                send(core_sem, core_in, who, part, mate, False, *valid)

    def from_y(d, base):
        for valid, step, _ in sides(d):
            arrive(ring_in, base + step, core, other_part, *valid)
            send(core_sem, core_in, base + step, other_part, mate, False, *valid)

    for d in range(1, nz + 2):
        if d < nz:
            from_z(d)
        if d == nz - 1:
            for j in range(1, n_dp):
                image(j).start()
        if d <= nz:
            from_x(d - 1)
        if 2 <= d <= nz:
            from_y(d - 1, dp)
        if d >= 2:
            from_y(d - 2, across)

    for who in range(n_dp):
        for part in range(PARTS):
            arrive(core_in, who, 1 - core, part)
    for j in range(1, n_dp):
        image_arrival(j).wait_recv()
    for conditions, wait in sent:
        when(conditions, wait)
    for j in range(1, n_dp):
        image(j).wait_send()
    own_image.wait()
    own_shard.wait()


def move_by_copies(patches, qkv_weight, table_len, table_dest):
    n_dp, n_core = lax.axis_size("dp"), lax.axis_size("fsdp")
    cap, width = patches.shape[0] // n_dp, patches.shape[1]
    columns = qkv_weight.shape[1]
    shard = qkv_weight.T.reshape(PARTS, columns // PARTS, width)
    dma = pltpu.SemaphoreType.DMA
    got, gathered = pl.pallas_call(
        functools.partial(move_kernel, n_dp, cap),
        in_specs=[
            pl.BlockSpec(memory_space=pltpu.SMEM),
            pl.BlockSpec(memory_space=pltpu.SMEM),
            pl.BlockSpec(memory_space=pltpu.VMEM),
            pl.BlockSpec(memory_space=pl.ANY),
        ],
        out_specs=[pl.BlockSpec(memory_space=pl.ANY)] * 2,
        out_shape=[
            jax.ShapeDtypeStruct((n_dp, cap, width), BF16),
            jax.ShapeDtypeStruct((n_dp, n_core, PARTS, columns // PARTS, width), BF16),
        ],
        scratch_shapes=[pltpu.VMEM((n_dp, cap, width), BF16)] + [dma((n_dp, PARTS))] * 7 + [dma((n_dp,))] * 2 + [dma((2,))],
        compiler_params=pltpu.CompilerParams(collective_id=0, has_side_effects=True, vmem_limit_bytes=40 * 2**20),
    )(table_len, table_dest, patches, shard)
    return got, gathered.reshape(n_dp * n_core * columns, width)


def on_device(patches, ln_gain, ln_bias, qkv_weight, qkv_bias, lengths, destinations):
    table_len, table_dest = lengths[0], destinations[0]
    by_copies = lax.axis_size("fsdp") == 2 and lax.axis_size("group") == 2 and lax.axis_size("dp") % 2 == 0
    got, weight_t = (move_by_copies if by_copies else move)(patches[0], qkv_weight, table_len, table_dest)
    context = attend(got, table_len, table_dest, ln_gain, ln_bias, weight_t, qkv_bias)
    return context.reshape(1, -1, context.shape[2])


def solution(mesh):
    placed = (
        P(("group", "fsdp"), "dp", None),
        P(),
        P(),
        P(None, ("dp", "fsdp")),
        P(),
        P(("group", "fsdp"), None, None),
        P(("group", "fsdp"), None, None),
    )
    return jax.shard_map(
        on_device,
        mesh=mesh,
        in_specs=placed,
        out_specs=P(("group", "fsdp"), "dp", None),
        check_vma=False,
    )
```

```python
import functools

import jax
import jax.numpy as jnp
from jax import lax
from jax.experimental import pallas as pl
from jax.experimental.pallas import tpu as pltpu
from jax.sharding import PartitionSpec as P

HEAD = 64
GROUP = 4
COLS = HEAD * GROUP
BF16 = jnp.bfloat16
F32 = jnp.float32


def attend_kernel(n_images, cap, table_len_ref, table_dest_ref, got_ref, gain_ref, shift_ref, bq_ref, bk_ref, bv_ref, wq_ref, wk_ref, wv_ref, out_ref, normed, len_ref):
    @pl.when(pl.program_id(0) == 0)
    def _():
        me = lax.axis_index("dp")
        for s in range(n_images):
            length = jnp.int32(0)
            for j in range(n_images):
                length = length + jnp.where(table_dest_ref[s, j] == me, table_len_ref[s, j], 0)
            len_ref[s] = length
        gain, shift = gain_ref[...][None, :], shift_ref[...][None, :]
        for s in range(0, n_images, 2):
            pair = []
            for x in (got_ref[s].astype(F32), got_ref[s + 1].astype(F32)):
                centred = x - jnp.mean(x, axis=1, keepdims=True)
                var = jnp.mean(centred * centred, axis=1, keepdims=True)
                pair.append(centred * lax.rsqrt(var + 1e-06) * gain + shift)
            normed[s * cap : (s + 2) * cap, :] = jnp.concatenate(pair, axis=0).astype(BF16)

    rows = normed[...]

    def project(w_ref, b_ref):
        y = lax.dot_general(rows, w_ref[...], (((1,), (1,)), ((), ())), preferred_element_type=F32)
        return (y + b_ref[...][None, :]).astype(BF16).astype(F32)

    q, k, v = project(wq_ref, bq_ref), project(wk_ref, bk_ref), project(wv_ref, bv_ref)
    lane_head = lax.broadcasted_iota(jnp.int32, (cap, COLS), 1) // HEAD
    key_at = lax.broadcasted_iota(jnp.int32, (cap, GROUP * cap), 0)
    row_at = lax.broadcasted_iota(jnp.int32, (cap, COLS), 0)
    for s in range(n_images):
        at = slice(s * cap, (s + 1) * cap)
        length = len_ref[s]
        stacked = jnp.concatenate([jnp.where(lane_head == h, q[at], 0.0) for h in range(GROUP)], axis=0)
        scores = lax.dot_general(k[at].astype(BF16), stacked.astype(BF16), (((1,), (1,)), ((), ())), preferred_element_type=F32)
        scores = jnp.where(key_at < length, scores * HEAD ** (-0.5), -1e30)
        expo = jnp.exp(scores - jnp.max(scores, axis=0, keepdims=True))
        probs = (expo * (1.0 / jnp.sum(expo, axis=0, keepdims=True))).astype(BF16)
        mixed = lax.dot_general(probs, v[at].astype(BF16), (((0,), (0,)), ((), ())), preferred_element_type=F32)
        total = jnp.where(lane_head == 0, mixed[:cap], 0.0)
        for h in range(1, GROUP):
            total = jnp.where(lane_head == h, mixed[h * cap : (h + 1) * cap], total)
        out_ref[s] = jnp.where(row_at < length, total, 0.0).astype(BF16)


def attend(got, table_len, table_dest, gain, shift, weight_t, bias):
    n_images, cap, width = got.shape
    steps = width // COLS
    full = lambda shape: pl.BlockSpec(shape, lambda i: (0,) * len(shape))
    bias_spec = lambda part: pl.BlockSpec((COLS,), lambda i: (part * steps + i,))
    weight_spec = lambda part: pl.BlockSpec((COLS, width), lambda i: (part * steps + i, 0))
    return pl.pallas_call(
        functools.partial(attend_kernel, n_images, cap),
        grid=(steps,),
        in_specs=[
            pl.BlockSpec(memory_space=pltpu.SMEM),
            pl.BlockSpec(memory_space=pltpu.SMEM),
            full((n_images, cap, width)),
            full((width,)),
            full((width,)),
            bias_spec(0),
            bias_spec(1),
            bias_spec(2),
            weight_spec(0),
            weight_spec(1),
            weight_spec(2),
        ],
        out_specs=pl.BlockSpec((n_images, cap, COLS), lambda i: (0, 0, i)),
        out_shape=jax.ShapeDtypeStruct((n_images, cap, width), BF16),
        scratch_shapes=[pltpu.VMEM((n_images * cap, width), BF16), pltpu.SMEM((n_images,), jnp.int32)],
        compiler_params=pltpu.CompilerParams(vmem_limit_bytes=48 * 2**20),
        cost_estimate=pl.CostEstimate(flops=2 * n_images * cap * width * 3 * width, bytes_accessed=3 * width * width * 2, transcendentals=0),
    )(table_len, table_dest, got, gain, shift, bias, bias, bias, weight_t, weight_t, weight_t)


def move(patches, qkv_weight, table_len, table_dest):
    n_dp = lax.axis_size("dp")
    me_dp = lax.axis_index("dp")
    cap, width = patches.shape[0] // n_dp, patches.shape[1]
    own_len = lax.dynamic_index_in_dim(table_len, me_dp, 0, keepdims=False)
    own_dest = lax.dynamic_index_in_dim(table_dest, me_dp, 0, keepdims=False)
    offsets = jnp.cumsum(own_len) - own_len
    onehot = own_dest[None, :] == jnp.arange(n_dp, dtype=jnp.int32)[:, None]
    slot_len = jnp.sum(jnp.where(onehot, own_len[None, :], 0), axis=1)
    slot_off = jnp.sum(jnp.where(onehot, offsets[None, :], 0), axis=1)
    position = jnp.arange(cap, dtype=jnp.int32)
    live = position[None, :] < slot_len[:, None]
    index = jnp.where(live, slot_off[:, None] + position[None, :], 0)
    picked = jnp.take(patches, index.reshape(-1), axis=0).reshape(n_dp, cap, width)
    outgoing = jnp.where(live[:, :, None], picked, jnp.zeros((), picked.dtype))
    got = lax.all_to_all(outgoing, "dp", split_axis=0, concat_axis=0, tiled=True)
    weight_t = lax.all_gather(qkv_weight.T, ("dp", "fsdp"), axis=0, tiled=True)
    return got, weight_t


MESH = pl.DeviceIdType.MESH
PARTS = 3


def move_kernel(n_dp, cap, len_ref, dest_ref, patches_ref, shard_ref, got_ref, all_ref, rows_ref, outgoing, up_sem, down_sem, x_sem, y_sem, core_sem, ring_in, core_in, image_out, image_in, local_sem):
    group, dp, core = lax.axis_index("group"), lax.axis_index("dp"), lax.axis_index("fsdp")
    nz = n_dp // 2
    z = dp // 2
    across = dp + 1 - 2 * (dp % 2)
    own_parts = (2 * group, 1)
    other_part = 2 - 2 * group
    replica = (1 - group, dp, core)
    mate = (group, dp, 1 - core)

    load = pltpu.make_async_copy(patches_ref, rows_ref, local_sem.at[2])
    load.start()
    barrier = pltpu.get_barrier_semaphore()
    for j in range(1, n_dp):
        pl.semaphore_signal(barrier, inc=1, device_id=(group, (dp + j) % n_dp, core), device_id_type=MESH)
    pl.semaphore_signal(barrier, inc=1, device_id=replica, device_id_type=MESH)
    pl.semaphore_signal(barrier, inc=1, device_id=mate, device_id_type=MESH)
    pl.semaphore_wait(barrier, n_dp + 1)

    sent = []

    def send(sems, into, who, part, device, own, *conditions):
        def copy():
            return pltpu.make_async_remote_copy(
                src_ref=shard_ref.at[part] if own else all_ref.at[who, core, part],
                dst_ref=all_ref.at[who, core, part],
                send_sem=sems.at[who, part],
                recv_sem=into.at[who, part],
                device_id=device,
                device_id_type=MESH,
            )

        when(conditions, lambda: copy().start())
        sent.append((conditions, lambda: copy().wait_send()))

    def when(conditions, do):
        if conditions:
            pl.when(conditions[0])(lambda: when(conditions[1:], do))
        else:
            do()

    def arrive(sems, who, of_core, part, *conditions):
        def wait():
            pltpu.make_async_remote_copy(
                src_ref=all_ref.at[who, of_core, part],
                dst_ref=all_ref.at[who, of_core, part],
                send_sem=y_sem.at[who, part],
                recv_sem=sems.at[who, part],
                device_id=mate,
                device_id_type=MESH,
            ).wait_recv()

        when(conditions, wait)

    for part in own_parts:
        send(up_sem, ring_in, dp, part, (group, dp + 2, core), True, z < nz - 1)
        send(down_sem, ring_in, dp, part, (group, dp - 2, core), True, z > 0)
        send(x_sem, ring_in, dp, part, (group, across, core), True)

    own_dest = [dest_ref[dp, i] for i in range(n_dp)]
    own_len = [len_ref[dp, i] for i in range(n_dp)]
    row_at = lax.broadcasted_iota(jnp.int32, (cap, n_dp * cap), 0)
    column_at = lax.broadcasted_iota(jnp.int32, (cap, n_dp * cap), 1)
    picks = []
    for j in range(n_dp):
        to = (dp + j) % n_dp
        length, offset, start = jnp.int32(0), jnp.int32(0), jnp.int32(0)
        for i in range(n_dp):
            length = jnp.where(own_dest[i] == to, own_len[i], length)
            offset = jnp.where(own_dest[i] == to, start, offset)
            start = start + own_len[i]
        picks.append(jnp.where((row_at < length) & (column_at == row_at + offset), 1.0, 0.0))
    pick = jnp.concatenate(picks, axis=0).astype(BF16)
    load.wait()
    picked = jnp.dot(pick, rows_ref[...], preferred_element_type=F32)
    for j in range(n_dp):
        outgoing[j] = picked[j * cap : (j + 1) * cap].astype(BF16)

    def image(j):
        return pltpu.make_async_remote_copy(
            src_ref=outgoing.at[j],
            dst_ref=got_ref.at[dp],
            send_sem=image_out.at[j],
            recv_sem=image_in.at[j],
            device_id=(group, (dp + j) % n_dp, core),
            device_id_type=MESH,
        )

    def image_arrival(j):
        source = (dp + n_dp - j) % n_dp
        return pltpu.make_async_remote_copy(
            src_ref=outgoing.at[j],
            dst_ref=got_ref.at[source],
            send_sem=image_out.at[j],
            recv_sem=image_in.at[j],
            device_id=(group, source, core),
            device_id_type=MESH,
        )

    own_image = pltpu.make_async_copy(outgoing.at[0], got_ref.at[dp], local_sem.at[0])
    own_image.start()
    own_shard = pltpu.make_async_copy(shard_ref, all_ref.at[dp, core], local_sem.at[1])
    own_shard.start()
    for part in range(PARTS):
        send(core_sem, core_in, dp, part, mate, True)

    def sides(d):
        if d == 0:
            return [((), 0, 0)]
        return [((z >= d,), -2 * d, 1), ((z < nz - d,), 2 * d, -1)]

    def from_z(d):
        for at, part in enumerate(own_parts):
            for valid, step, way in sides(d):
                who = dp + step
                arrive(ring_in, who, core, part, *valid)
                if way == 1:
                    send(up_sem, ring_in, who, part, (group, dp + 2, core), False, *valid, z < nz - 1)
                else:
                    send(down_sem, ring_in, who, part, (group, dp - 2, core), False, *valid, z > 0)
                send(x_sem, ring_in, who, part, (group, across, core), False, *valid)
                if at == 0:
                    send(y_sem, ring_in, who, part, replica, False, *valid)
                send(core_sem, core_in, who, part, mate, False, *valid)

    def from_x(d):
        for at, part in enumerate(own_parts):
            for valid, step, _ in sides(d):
                who = across + step
                arrive(ring_in, who, core, part, *valid)
                if at == 0:
                    send(y_sem, ring_in, who, part, replica, False, *valid)
                send(core_sem, core_in, who, part, mate, False, *valid)

    def from_y(d, base):
        for valid, step, _ in sides(d):
            arrive(ring_in, base + step, core, other_part, *valid)
            send(core_sem, core_in, base + step, other_part, mate, False, *valid)

    for d in range(1, nz + 2):
        if d < nz:
            from_z(d)
        if d == nz - 1:
            for j in range(1, n_dp):
                image(j).start()
        if d <= nz:
            from_x(d - 1)
        if 2 <= d <= nz:
            from_y(d - 1, dp)
        if d >= 2:
            from_y(d - 2, across)

    for who in range(n_dp):
        for part in range(PARTS):
            arrive(core_in, who, 1 - core, part)
    for j in range(1, n_dp):
        image_arrival(j).wait_recv()
    for conditions, wait in sent:
        when(conditions, wait)
    for j in range(1, n_dp):
        image(j).wait_send()
    own_image.wait()
    own_shard.wait()


def move_by_copies(patches, qkv_weight, table_len, table_dest):
    n_dp, n_core = lax.axis_size("dp"), lax.axis_size("fsdp")
    cap, width = patches.shape[0] // n_dp, patches.shape[1]
    columns = qkv_weight.shape[1]
    shard = qkv_weight.T.reshape(PARTS, columns // PARTS, width)
    dma = pltpu.SemaphoreType.DMA
    got, gathered = pl.pallas_call(
        functools.partial(move_kernel, n_dp, cap),
        in_specs=[
            pl.BlockSpec(memory_space=pltpu.SMEM),
            pl.BlockSpec(memory_space=pltpu.SMEM),
            pl.BlockSpec(memory_space=pl.ANY),
            pl.BlockSpec(memory_space=pl.ANY),
        ],
        out_specs=[pl.BlockSpec(memory_space=pl.ANY)] * 2,
        out_shape=[
            jax.ShapeDtypeStruct((n_dp, cap, width), BF16),
            jax.ShapeDtypeStruct((n_dp, n_core, PARTS, columns // PARTS, width), BF16),
        ],
        scratch_shapes=[pltpu.VMEM((n_dp * cap, width), BF16), pltpu.VMEM((n_dp, cap, width), BF16)] + [dma((n_dp, PARTS))] * 7 + [dma((n_dp,))] * 2 + [dma((3,))],
        compiler_params=pltpu.CompilerParams(collective_id=0, has_side_effects=True, vmem_limit_bytes=40 * 2**20),
    )(table_len, table_dest, patches, shard)
    return got, gathered.reshape(n_dp * n_core * columns, width)


def on_device(patches, ln_gain, ln_bias, qkv_weight, qkv_bias, lengths, destinations):
    table_len, table_dest = lengths[0], destinations[0]
    by_copies = lax.axis_size("fsdp") == 2 and lax.axis_size("group") == 2 and lax.axis_size("dp") % 2 == 0
    got, weight_t = (move_by_copies if by_copies else move)(patches[0], qkv_weight, table_len, table_dest)
    context = attend(got, table_len, table_dest, ln_gain, ln_bias, weight_t, qkv_bias)
    return context.reshape(1, -1, context.shape[2])


def solution(mesh):
    placed = (
        P(("group", "fsdp"), "dp", None),
        P(),
        P(),
        P(None, ("dp", "fsdp")),
        P(),
        P(("group", "fsdp"), None, None),
        P(("group", "fsdp"), None, None),
    )
    return jax.shard_map(
        on_device,
        mesh=mesh,
        in_specs=placed,
        out_specs=P(("group", "fsdp"), "dp", None),
        check_vma=False,
    )
```
